32 devices in a mesh: cols: 4 (over x, core), rows: 8 (over z, y).
Axes of the slice: x: 2, y: 2, z: 4, core: 2. Of those that a mesh axis runs over, the one named last changes fastest.
Arguments:
- snapshots: float32 [8192, 512], P('rows', 'cols')
- plan: int32 [3], replicated, may hold values from 1 to 3, as said below
Outputs:
- rotated: float32 [8192, 512], P('rows', 'cols')
The draws below stay inside these ranges and needn't reach their ends.
Inputs may be any that keep to these rules, and one draw needn't show every extreme that they name: `plan`: the 3 masks are distinct; among them are 3 and 2.
All inputs are finite; a program needn't handle non-finite values.
Results may differ from the reference program's by a relative error of at most 0.0003.
Values sent between devices are 32-bit elements; how exact they have to be, the bound alone decides.
A program may use at most 64 MiB of HBM per device.

```python
import jax
import jax.numpy as jnp
from jax import lax

BC = 128
ITERS = 3
NSI = 5
NBLK = 4
COLS = 512
M = 8192


def draw_snapshots(key, part):
    key_noise = jax.random.fold_in(key, 11)
    key_shared = jax.random.fold_in(key, 12)
    key_weight = jax.random.fold_in(key, 13)
    shared = jax.random.normal(key_shared, (M, 1), jnp.float32)
    weights = jax.random.uniform(key_weight, (1, COLS), jnp.float32, 0.5, 1.5)
    noise = jax.random.normal(key_noise, (M, COLS), jnp.float32)
    return noise + 0.3 * shared * weights


def draw_plan(key, part):
    key_perm = jax.random.fold_in(key, 21)
    key_order = jax.random.fold_in(key, 22)
    values = jnp.arange(1, NBLK, dtype=jnp.int32)
    scores = jax.random.permutation(key_perm, jnp.arange(NBLK - 1, dtype=jnp.int32))
    special = jnp.logical_or(values == NBLK - 1, values == NBLK // 2)
    scores = scores + jnp.where(special, NBLK, 0).astype(jnp.int32)
    top_scores, top_index = lax_top(scores)
    chosen = values[top_index]
    shuffle = jax.random.permutation(key_order, jnp.arange(ITERS, dtype=jnp.int32))
    return chosen[shuffle].astype(jnp.int32)


def lax_top(scores):
    return jax.lax.top_k(scores, ITERS)


def setup_inputs(seed: int = 0) -> dict:
    key_of = jax.random.split(jax.random.key(seed), 3)
    return {
        "snapshots": draw_snapshots(jax.random.fold_in(key_of[2], 71), 0),
        "plan": draw_plan(jax.random.fold_in(key_of[2], 71), 0),
    }


def rotation(gram, sign):
    half = gram.shape[0] // 2
    diag = jnp.diagonal(gram)
    cross = gram[:half, half:] / jnp.sqrt(jnp.outer(diag[:half] + 1e-06, diag[half:] + 1e-06))
    gen = sign * cross / jnp.sqrt(1.0 + jnp.sum(cross * cross))
    zero = jnp.zeros((half, half), jnp.float32)
    top = jnp.concatenate([zero, -gen], axis=1)
    bottom = jnp.concatenate([gen.T, zero], axis=1)
    eye = jnp.eye(2 * half, dtype=jnp.float32)
    ymat = (eye + jnp.concatenate([top, bottom], axis=0)) / jnp.sqrt(jnp.float32(2.0))
    for index in range(NSI):
        inner = jnp.dot(ymat.T, ymat, precision=lax.Precision.HIGHEST)
        ymat = 1.5 * ymat - 0.5 * jnp.dot(ymat, inner, precision=lax.Precision.HIGHEST)
    return ymat

def reference(snapshots, plan):
    blocks = snapshots.reshape(M, NBLK, BC)
    labels = jnp.arange(NBLK, dtype=jnp.int32)
    hi = lax.Precision.HIGHEST
    for step in range(ITERS):
        partner = jnp.bitwise_xor(labels, plan[step])
        sign = jnp.where(labels < partner, 1.0, -1.0).astype(jnp.float32)
        other = blocks[:, partner, :]
        own_own = jnp.einsum('mbi,mbj->bij', blocks, blocks, precision=hi)
        own_other = jnp.einsum('mbi,mbj->bij', blocks, other, precision=hi)
        other_own = jnp.einsum('mbi,mbj->bij', other, blocks, precision=hi)
        other_other = own_own[partner]
        gram = jnp.concatenate([jnp.concatenate([own_own, own_other], axis=2), jnp.concatenate([other_own, other_other], axis=2)], axis=1)
        rot = jax.vmap(rotation)(gram, sign)
        blocks = jnp.einsum('mbi,bij->mbj', blocks, rot[:, :BC, :BC], precision=hi) + jnp.einsum('mbi,bij->mbj', other, rot[:, BC:, :BC], precision=hi)
    return blocks.reshape(M, COLS)
```

```python
import functools

import jax
import jax.numpy as jnp
from jax import lax
from jax.experimental import pallas as pl
from jax.experimental.pallas import tpu as pltpu
from jax.sharding import PartitionSpec as P

NSI = 5
EPS = 1e-6
VMEM = pl.BlockSpec(memory_space=pltpu.VMEM)
SMEM = pl.BlockSpec(memory_space=pltpu.SMEM)


def split(x):
    high = x.astype(jnp.bfloat16)
    return high, (x - high.astype(jnp.float32)).astype(jnp.bfloat16)


def dots(a, b, ca=1, cb=0):
    def one(x, y):
        return lax.dot_general(
            x, y, (((ca,), (cb,)), ((), ())), preferred_element_type=jnp.float32
        )

    return one(a[0], b[0]) + (one(a[0], b[1]) + one(a[1], b[0]))


def dot(a, b, ca=1, cb=0):
    return dots(split(a), split(b), ca, cb)


def columns(gens):
    width = gens[0].shape[0]
    row = lax.broadcasted_iota(jnp.int32, (width, width), 0)
    col = lax.broadcasted_iota(jnp.int32, (width, width), 1)
    eye = jnp.where(row == col, 1.0, 0.0).astype(jnp.float32)
    parts = [split(g) for g in gens]
    zs = [0.5 * (eye + dots(p, p, 1, 1)) for p in parts]
    qs = None
    for index in range(NSI):
        ts = [1.5 * eye - 0.5 * z for z in zs]
        tsp = [split(t) for t in ts]
        if qs is None:
            qs = [t * (0.5**0.5) for t in ts]
        else:
            qs = [dots(split(q), t) for q, t in zip(qs, tsp)]
        if index < NSI - 1:
            squares = [dots(t, t) for t in tsp]
            zs = [dot(z, s) for z, s in zip(zs, squares)]
    return [(q, dots(p, split(q), 0, 0)) for q, p in zip(qs, parts)]


def generator(cross, own, other, sign):
    width = cross.shape[0]
    row = lax.broadcasted_iota(jnp.int32, (width, width), 0)
    col = lax.broadcasted_iota(jnp.int32, (width, width), 1)
    diag = row == col
    dc = jnp.sum(jnp.where(diag, own, 0.0), axis=1, keepdims=True)
    dp = jnp.sum(jnp.where(diag, other, 0.0), axis=0, keepdims=True)
    dc = jnp.maximum(dc, 0.0) + EPS
    dp = jnp.maximum(dp, 0.0) + EPS
    cross = cross * (lax.rsqrt(dc) * lax.rsqrt(dp))
    total = jnp.sum(jnp.sum(cross * cross, axis=1, keepdims=True), axis=0, keepdims=True)
    return cross * (sign * lax.rsqrt(1.0 + total))


def rotate_kernel(nb, plan_ref, label_ref, gram_ref, all_ref, out_ref):
    width = out_ref.shape[1]
    label = label_ref[0]
    masks = [plan_ref[s] for s in range(3)]
    labels = []
    for slot in range(8):
        block = label
        for bit in range(3):
            if slot >> bit & 1:
                block = jnp.bitwise_xor(block, masks[bit])
        labels.append(block)

    def sign(i, j):
        return jnp.where(labels[i] < labels[j], 1.0, -1.0).astype(jnp.float32)

    loaded = {}

    def gram(i, j):
        if (i, j) not in loaded:
            at = pl.multiple_of(labels[j] * width, width)
            loaded[i, j] = gram_ref[labels[i], :, pl.ds(at, width)]
        return loaded[i, j]

    def stack(parts, axis):
        return jnp.concatenate(parts, axis=axis)

    outs = (0, 2, 4, 6)
    gens = [generator(gram(i, i + 1), gram(i, i), gram(i + 1, i + 1), sign(i, i + 1)) for i in outs]
    first = columns(gens)
    col = {i: split(stack(c, 0)) for i, c in zip(outs, first)}
    after = {}
    for i in outs:
        for j in outs:
            if j < i:
                continue
            wide = stack(
                [stack([gram(i + p, j), gram(i + p, j + 1)], 1) for p in (0, 1)], 0
            )
            half = dots(split(wide), col[j])
            after[i, j] = dots(col[i], split(half), 0, 0)

    gens = [generator(after[i, i + 2], after[i, i], after[i + 2, i + 2], sign(i, i + 2)) for i in (0, 4)]
    second = columns(gens)
    c0, c4 = [split(stack(c, 0)) for c in second]

    def block(i, j):
        return stack(
            [
                stack([after[i, j], after[i, j + 2]], 1),
                stack([after[i + 2, j] if i + 2 <= j else after[j, i + 2].T, after[i + 2, j + 2]], 1),
            ],
            0,
        )

    def update(ci, mat, cj):
        return dots(ci, split(dots(split(mat), cj)), 0, 0)

    g00 = update(c0, block(0, 0), c0)
    g04 = update(c0, block(0, 4), c4)
    g44 = update(c4, block(4, 4), c4)
    gens = [generator(g04, g00, g44, sign(0, 4))]
    (a, b), = columns(gens)
    top = dots(c0, split(a))
    bottom = dots(c4, split(b))
    weight = {0: top[:width], 2: top[width:], 4: bottom[:width], 6: bottom[width:]}
    coef = {}
    for i in outs:
        both = dots(col[i], split(weight[i]))
        coef[i], coef[i + 1] = both[:width], both[width:]
    slots = range(8)
    if nb == 4:
        coef = {k: coef[k] + coef[7 - k] for k in range(4)}
        slots = range(4)
    coefs = [split(coef[k]) for k in slots]
    rows = out_ref.shape[0]
    tile = min(rows, 256)

    @pl.loop(0, rows // tile)
    def _(t):
        at = pl.multiple_of(t * tile, tile)
        total = jnp.zeros((tile, width), jnp.float32)
        for k in range(len(coefs)):
            total += dots(split(all_ref[labels[k], pl.ds(at, tile), :]), coefs[k])
        out_ref[pl.ds(at, tile), :] = total


def rotate(nb, plan, label, gram, blocks):
    rows, width = blocks.shape[1:]
    return pl.pallas_call(
        functools.partial(rotate_kernel, nb),
        out_shape=jax.ShapeDtypeStruct((rows, width), jnp.float32),
        in_specs=[SMEM, SMEM, VMEM, VMEM],
        out_specs=VMEM,
        compiler_params=pltpu.CompilerParams(vmem_limit_bytes=48 * 2**20),
    )(plan, label, gram, blocks)


def local(nb, snapshots, plan):
    label = lax.axis_index("cols").astype(jnp.int32)
    blocks = lax.all_gather(snapshots, "cols", axis=0)
    width = snapshots.shape[1]
    panel = jnp.einsum("mi,bmj->ibj", snapshots, blocks, precision=lax.Precision.HIGH)
    panel = lax.psum(panel.reshape(width, nb * width), "rows")
    gram = lax.all_gather(panel, "cols", axis=0)
    return rotate(nb, plan, label.reshape(1), gram, blocks)


def solution(mesh):
    return jax.shard_map(
        functools.partial(local, mesh.shape["cols"]),
        mesh=mesh,
        in_specs=(P("rows", "cols"), P()),
        out_specs=P("rows", "cols"),
        check_vma=False,
    )
```

```python
import functools

import jax
import jax.numpy as jnp
from jax import lax
from jax.experimental import pallas as pl
from jax.experimental.pallas import tpu as pltpu
from jax.sharding import PartitionSpec as P

NSI = 5
EPS = 1e-6
VMEM = pl.BlockSpec(memory_space=pltpu.VMEM)
MESH = pl.DeviceIdType.MESH
SMEM = pl.BlockSpec(memory_space=pltpu.SMEM)


def split(x):
    high = x.astype(jnp.bfloat16)
    return high, (x - high.astype(jnp.float32)).astype(jnp.bfloat16)


def dots(a, b, ca=1, cb=0):
    def one(x, y):
        return lax.dot_general(
            x, y, (((ca,), (cb,)), ((), ())), preferred_element_type=jnp.float32
        )

    return one(a[0], b[0]) + (one(a[0], b[1]) + one(a[1], b[0]))


def dot(a, b, ca=1, cb=0):
    return dots(split(a), split(b), ca, cb)


def columns(gens):
    width = gens[0].shape[0]
    row = lax.broadcasted_iota(jnp.int32, (width, width), 0)
    col = lax.broadcasted_iota(jnp.int32, (width, width), 1)
    eye = jnp.where(row == col, 1.0, 0.0).astype(jnp.float32)
    parts = [split(g) for g in gens]
    zs = [0.5 * (eye + dots(p, p, 1, 1)) for p in parts]
    qs = None
    for index in range(NSI):
        ts = [1.5 * eye - 0.5 * z for z in zs]
        tsp = [split(t) for t in ts]
        if qs is None:
            qs = [t * (0.5**0.5) for t in ts]
        else:
            qs = [dots(split(q), t) for q, t in zip(qs, tsp)]
        if index < NSI - 1:
            squares = [dots(t, t) for t in tsp]
            zs = [dot(z, s) for z, s in zip(zs, squares)]
    return [(q, dots(p, split(q), 0, 0)) for q, p in zip(qs, parts)]


def generator(cross, own, other, sign):
    width = cross.shape[0]
    row = lax.broadcasted_iota(jnp.int32, (width, width), 0)
    col = lax.broadcasted_iota(jnp.int32, (width, width), 1)
    diag = row == col
    dc = jnp.sum(jnp.where(diag, own, 0.0), axis=1, keepdims=True)
    dp = jnp.sum(jnp.where(diag, other, 0.0), axis=0, keepdims=True)
    dc = jnp.maximum(dc, 0.0) + EPS
    dp = jnp.maximum(dp, 0.0) + EPS
    cross = cross * (lax.rsqrt(dc) * lax.rsqrt(dp))
    total = jnp.sum(jnp.sum(cross * cross, axis=1, keepdims=True), axis=0, keepdims=True)
    return cross * (sign * lax.rsqrt(1.0 + total))


def rotate_kernel(nb, plan_ref, label_ref, gram_ref, all_ref, out_ref):
    width = out_ref.shape[1]
    label = label_ref[0]
    masks = [plan_ref[s] for s in range(3)]
    labels = []
    for slot in range(8):
        block = label
        for bit in range(3):
            if slot >> bit & 1:
                block = jnp.bitwise_xor(block, masks[bit])
        labels.append(block)

    def sign(i, j):
        return jnp.where(labels[i] < labels[j], 1.0, -1.0).astype(jnp.float32)

    loaded = {}

    def gram(i, j):
        if (i, j) not in loaded:
            at = pl.multiple_of(labels[i] * width, width)
            loaded[i, j] = gram_ref[labels[j], pl.ds(at, width), :]
        return loaded[i, j]

    def stack(parts, axis):
        return jnp.concatenate(parts, axis=axis)

    outs = (0, 2, 4, 6)
    gens = [generator(gram(i, i + 1), gram(i, i), gram(i + 1, i + 1), sign(i, i + 1)) for i in outs]
    first = columns(gens)
    col = {i: split(stack(c, 0)) for i, c in zip(outs, first)}
    after = {}
    for i in outs:
        for j in outs:
            if j < i:
                continue
            wide = stack(
                [stack([gram(i + p, j), gram(i + p, j + 1)], 1) for p in (0, 1)], 0
            )
            half = dots(split(wide), col[j])
            after[i, j] = dots(col[i], split(half), 0, 0)

    gens = [generator(after[i, i + 2], after[i, i], after[i + 2, i + 2], sign(i, i + 2)) for i in (0, 4)]
    second = columns(gens)
    c0, c4 = [split(stack(c, 0)) for c in second]

    def block(i, j):
        return stack(
            [
                stack([after[i, j], after[i, j + 2]], 1),
                stack([after[i + 2, j] if i + 2 <= j else after[j, i + 2].T, after[i + 2, j + 2]], 1),
            ],
            0,
        )

    def update(ci, mat, cj):
        return dots(ci, split(dots(split(mat), cj)), 0, 0)

    g00 = update(c0, block(0, 0), c0)
    g04 = update(c0, block(0, 4), c4)
    g44 = update(c4, block(4, 4), c4)
    gens = [generator(g04, g00, g44, sign(0, 4))]
    (a, b), = columns(gens)
    top = dots(c0, split(a))
    bottom = dots(c4, split(b))
    weight = {0: top[:width], 2: top[width:], 4: bottom[:width], 6: bottom[width:]}
    coef = {}
    for i in outs:
        both = dots(col[i], split(weight[i]))
        coef[i], coef[i + 1] = both[:width], both[width:]
    slots = range(8)
    if nb == 4:
        coef = {k: coef[k] + coef[7 - k] for k in range(4)}
        slots = range(4)
    coefs = [split(coef[k]) for k in slots]
    rows = out_ref.shape[0]
    tile = min(rows, 256)

    @pl.loop(0, rows // tile)
    def _(t):
        at = pl.multiple_of(t * tile, tile)
        total = jnp.zeros((tile, width), jnp.float32)
        for k in range(len(coefs)):
            total += dots(split(all_ref[labels[k], pl.ds(at, tile), :]), coefs[k])
        out_ref[pl.ds(at, tile), :] = total


def rotate(nb, plan, label, gram, blocks):
    rows, width = blocks.shape[1:]
    return pl.pallas_call(
        functools.partial(rotate_kernel, nb),
        out_shape=jax.ShapeDtypeStruct((rows, width), jnp.float32),
        in_specs=[SMEM, SMEM, VMEM, VMEM],
        out_specs=VMEM,
        compiler_params=pltpu.CompilerParams(vmem_limit_bytes=48 * 2**20),
    )(plan, label, gram, blocks)


def gather_kernel(nb, nr, own_ref, all_ref, gram_ref, part, land, *sems):
    a_send, a_recv, b_send, b_recv, c_send, c_recv, d_send, d_recv = sems
    me, row = lax.axis_index("cols"), lax.axis_index("rows")
    chips = nb // 2
    chip, core = me // 2, lax.rem(me, 2)
    sibling = chip * 2 + (1 - core)
    rows, width = own_ref.shape
    piece = nb * width // nr
    far = range(1, chips)

    def ahead(d):
        return lax.rem(chip + d, chips)

    def behind(d):
        return lax.rem(chip + chips - d, chips)

    def peer(k):
        return lax.rem(row + k, nr)

    barrier = pltpu.get_barrier_semaphore()
    targets = [{"cols": sibling}] + [{"cols": ahead(d) * 2 + core} for d in far]
    targets += [{"rows": peer(k)} for k in range(1, nr)]
    for target in targets:
        pl.semaphore_signal(barrier, inc=1, device_id=target, device_id_type=MESH)
    pl.semaphore_wait(barrier, len(targets))

    def gather(ref, source, send, recv, chunks, arrived):
        size = ref.shape[1] // chunks

        def direct(d, ch):
            at = pl.ds(ch * size, size)
            return pltpu.make_async_remote_copy(
                source.at[at], ref.at[me, at], send.at[d, 0, ch], recv.at[d, 0, ch],
                device_id={"cols": ahead(d) * 2 + core}, device_id_type=MESH,
            )

        def relay(d, ch):
            at = pl.ds(ch * size, size)
            block = behind(d) * 2 + core
            return pltpu.make_async_remote_copy(
                source.at[at] if d == 0 else ref.at[block, at], ref.at[block, at],
                send.at[d, 1, ch], recv.at[d, 1, ch],
                device_id={"cols": sibling}, device_id_type=MESH,
            )

        copies = []

        def start(copy):
            copy.start()
            copies.append(copy)

        for ch in range(chunks):
            for d in far:
                start(direct(d, ch))
        for ch in range(chunks):
            start(relay(0, ch))
        for ch in range(chunks):
            arrived(me, ch, size)
        for ch in range(chunks):
            relay(0, ch).wait_recv()
            arrived(sibling, ch, size)
        for ch in range(chunks + 1):
            for d in far:
                if ch < chunks:
                    direct(d, ch).wait_recv()
                    start(relay(d, ch))
                    arrived(behind(d) * 2 + core, ch, size)
                if ch > 0:
                    relay(d, ch - 1).wait_recv()
                    arrived(behind(d) * 2 + 1 - core, ch - 1, size)
        return copies

    def multiply(block, ch, size):
        at = pl.ds(ch * size, size)
        to = pl.ds(pl.multiple_of(block * width, width), width)
        product = dot(all_ref[block, at, :], own_ref[at, :], 0, 0)
        if ch == 0:
            part[to, :] = product
        else:
            part[to, :] += product

    all_ref[me] = own_ref[...]
    started = gather(all_ref, own_ref, a_send, a_recv, a_send.shape[2], multiply)

    def scatter(k):
        return pltpu.make_async_remote_copy(
            part.at[pl.ds(pl.multiple_of(peer(k) * piece, piece), piece)], land.at[k - 1],
            b_send.at[k - 1], b_recv.at[k - 1],
            device_id={"rows": peer(k)}, device_id_type=MESH,
        )

    mine = pl.ds(pl.multiple_of(row * piece, piece), piece)

    def spread(k):
        return pltpu.make_async_remote_copy(
            gram_ref.at[me, mine], gram_ref.at[me, mine], c_send.at[k - 1], c_recv.at[k - 1],
            device_id={"rows": peer(k)}, device_id_type=MESH,
        )

    for make in (scatter, spread):
        for k in range(1, nr):
            copy = make(k)
            copy.start()
            started.append(copy)
        if make is scatter:
            total = part[mine, :]
            for k in range(1, nr):
                scatter(k).wait_recv()
                total += land[k - 1]
            gram_ref[me, mine, :] = total
    for k in range(1, nr):
        spread(k).wait_recv()
    started += gather(
        gram_ref, gram_ref.at[me], d_send, d_recv, d_send.shape[2], lambda *_: None
    )
    for copy in started:
        copy.wait_send()


def gather(nb, nr, snapshots):
    rows, width = snapshots.shape
    chips = nb // 2
    dma = pltpu.SemaphoreType.DMA
    return pl.pallas_call(
        functools.partial(gather_kernel, nb, nr),
        out_shape=(
            jax.ShapeDtypeStruct((nb, rows, width), jnp.float32),
            jax.ShapeDtypeStruct((nb, nb * width, width), jnp.float32),
        ),
        in_specs=[VMEM],
        out_specs=(VMEM, VMEM),
        scratch_shapes=[
            pltpu.VMEM((nb * width, width), jnp.float32),
            pltpu.VMEM((nr - 1, nb * width // nr, width), jnp.float32),
            dma((chips, 2, 4)), dma((chips, 2, 4)),
            dma((nr - 1,)), dma((nr - 1,)),
            dma((nr - 1,)), dma((nr - 1,)),
            dma((chips, 2, 2)), dma((chips, 2, 2)),
        ],
        compiler_params=pltpu.CompilerParams(
            collective_id=0, has_side_effects=True, vmem_limit_bytes=48 * 2**20
        ),
    )(snapshots)


def local(nb, nr, snapshots, plan):
    label = lax.axis_index("cols").astype(jnp.int32)
    blocks, gram = gather(nb, nr, snapshots)
    return rotate(nb, plan, label.reshape(1), gram, blocks)


def solution(mesh):
    return jax.shard_map(
        functools.partial(local, mesh.shape["cols"], mesh.shape["rows"]),
        mesh=mesh,
        in_specs=(P("rows", "cols"), P()),
        out_specs=P("rows", "cols"),
        check_vma=False,
    )
```

```python
import functools

import jax
import jax.numpy as jnp
from jax import lax
from jax.experimental import pallas as pl
from jax.experimental.pallas import tpu as pltpu
from jax.sharding import PartitionSpec as P

NSI = 5
EPS = 1e-6
VMEM = pl.BlockSpec(memory_space=pltpu.VMEM)
MESH = pl.DeviceIdType.MESH
SMEM = pl.BlockSpec(memory_space=pltpu.SMEM)


def split(x):
    high = x.astype(jnp.bfloat16)
    return high, (x - high.astype(jnp.float32)).astype(jnp.bfloat16)


def dots(a, b, ca=1, cb=0):
    def one(x, y):
        return lax.dot_general(
            x, y, (((ca,), (cb,)), ((), ())), preferred_element_type=jnp.float32
        )

    return one(a[0], b[0]) + (one(a[0], b[1]) + one(a[1], b[0]))


def dot(a, b, ca=1, cb=0):
    return dots(split(a), split(b), ca, cb)


def columns(gens):
    width = gens[0].shape[0]
    row = lax.broadcasted_iota(jnp.int32, (width, width), 0)
    col = lax.broadcasted_iota(jnp.int32, (width, width), 1)
    eye = jnp.where(row == col, 1.0, 0.0).astype(jnp.float32)
    parts = [split(g) for g in gens]
    zs = [0.5 * (eye + dots(p, p, 1, 1)) for p in parts]
    qs = None
    for index in range(NSI):
        ts = [1.5 * eye - 0.5 * z for z in zs]
        tsp = [split(t) for t in ts]
        if qs is None:
            qs = [t * (0.5**0.5) for t in ts]
        else:
            qs = [dots(split(q), t) for q, t in zip(qs, tsp)]
        if index < NSI - 1:
            squares = [dots(t, t) for t in tsp]
            zs = [dot(z, s) for z, s in zip(zs, squares)]
    return [(q, dots(p, split(q), 0, 0)) for q, p in zip(qs, parts)]


def generator(cross, own, other, sign):
    width = cross.shape[0]
    row = lax.broadcasted_iota(jnp.int32, (width, width), 0)
    col = lax.broadcasted_iota(jnp.int32, (width, width), 1)
    diag = row == col
    dc = jnp.sum(jnp.where(diag, own, 0.0), axis=1, keepdims=True)
    dp = jnp.sum(jnp.where(diag, other, 0.0), axis=0, keepdims=True)
    dc = jnp.maximum(dc, 0.0) + EPS
    dp = jnp.maximum(dp, 0.0) + EPS
    cross = cross * (lax.rsqrt(dc) * lax.rsqrt(dp))
    total = jnp.sum(jnp.sum(cross * cross, axis=1, keepdims=True), axis=0, keepdims=True)
    return cross * (sign * lax.rsqrt(1.0 + total))


def rotate_kernel(nb, plan_ref, label_ref, gram_ref, all_ref, out_ref):
    width = out_ref.shape[1]
    label = label_ref[0]
    masks = [plan_ref[s] for s in range(3)]
    labels = []
    for slot in range(8):
        block = label
        for bit in range(3):
            if slot >> bit & 1:
                block = jnp.bitwise_xor(block, masks[bit])
        labels.append(block)

    def sign(i, j):
        return jnp.where(labels[i] < labels[j], 1.0, -1.0).astype(jnp.float32)

    loaded = {}

    def gram(i, j):
        if (i, j) not in loaded:
            at = pl.multiple_of(labels[i] * width, width)
            loaded[i, j] = gram_ref[labels[j], pl.ds(at, width), :]
        return loaded[i, j]

    def stack(parts, axis):
        return jnp.concatenate(parts, axis=axis)

    outs = (0, 2, 4, 6)
    gens = [generator(gram(i, i + 1), gram(i, i), gram(i + 1, i + 1), sign(i, i + 1)) for i in outs]
    first = columns(gens)
    col = {i: split(stack(c, 0)) for i, c in zip(outs, first)}
    after = {}
    for i in outs:
        for j in outs:
            if j < i:
                continue
            wide = stack(
                [stack([gram(i + p, j), gram(i + p, j + 1)], 1) for p in (0, 1)], 0
            )
            half = dots(split(wide), col[j])
            after[i, j] = dots(col[i], split(half), 0, 0)

    gens = [generator(after[i, i + 2], after[i, i], after[i + 2, i + 2], sign(i, i + 2)) for i in (0, 4)]
    second = columns(gens)
    c0, c4 = [split(stack(c, 0)) for c in second]

    def block(i, j):
        return stack(
            [
                stack([after[i, j], after[i, j + 2]], 1),
                stack([after[i + 2, j] if i + 2 <= j else after[j, i + 2].T, after[i + 2, j + 2]], 1),
            ],
            0,
        )

    def update(ci, mat, cj):
        return dots(ci, split(dots(split(mat), cj)), 0, 0)

    g00 = update(c0, block(0, 0), c0)
    g04 = update(c0, block(0, 4), c4)
    g44 = update(c4, block(4, 4), c4)
    gens = [generator(g04, g00, g44, sign(0, 4))]
    (a, b), = columns(gens)
    top = dots(c0, split(a))
    bottom = dots(c4, split(b))
    weight = {0: top[:width], 2: top[width:], 4: bottom[:width], 6: bottom[width:]}
    coef = {}
    for i in outs:
        both = dots(col[i], split(weight[i]))
        coef[i], coef[i + 1] = both[:width], both[width:]
    slots = range(8)
    if nb == 4:
        coef = {k: coef[k] + coef[7 - k] for k in range(4)}
        slots = range(4)
    coefs = [split(coef[k]) for k in slots]
    rows = out_ref.shape[0]
    tile = min(rows, 256)

    @pl.loop(0, rows // tile)
    def _(t):
        at = pl.multiple_of(t * tile, tile)
        total = jnp.zeros((tile, width), jnp.float32)
        for k in range(len(coefs)):
            total += dots(split(all_ref[labels[k], pl.ds(at, tile), :]), coefs[k])
        out_ref[pl.ds(at, tile), :] = total


def rotate(nb, plan, label, gram, blocks):
    rows, width = blocks.shape[1:]
    return pl.pallas_call(
        functools.partial(rotate_kernel, nb),
        out_shape=jax.ShapeDtypeStruct((rows, width), jnp.float32),
        in_specs=[SMEM, SMEM, VMEM, VMEM],
        out_specs=VMEM,
        compiler_params=pltpu.CompilerParams(vmem_limit_bytes=48 * 2**20),
    )(plan, label, gram, blocks)


def gather_kernel(nb, nr, own_ref, all_ref, gram_ref, part, land, *sems):
    a_send, a_recv, b_send, b_recv, c_send, c_recv, d_send, d_recv = sems
    me, row = lax.axis_index("cols"), lax.axis_index("rows")
    chips = nb // 2
    chip, core = me // 2, lax.rem(me, 2)
    sibling = chip * 2 + (1 - core)
    rows, width = own_ref.shape
    piece = 2 * width // nr
    far = range(1, chips)
    chunks = a_send.shape[2]
    size = rows // chunks

    def ahead(d):
        return lax.rem(chip + d, chips)

    def behind(d):
        return lax.rem(chip + 2 * chips - d, chips)

    def peer(k):
        return lax.rem(row + k, nr)

    barrier = pltpu.get_barrier_semaphore()
    targets = [{"cols": sibling}] + [{"cols": ahead(d) * 2 + core} for d in far]
    targets += [{"rows": peer(k)} for k in range(1, nr)]
    for target in targets:
        pl.semaphore_signal(barrier, inc=1, device_id=target, device_id_type=MESH)
    pl.semaphore_wait(barrier, len(targets))

    started = []

    def start(copy):
        copy.start()
        started.append(copy)

    def copies(ref, source, send, recv, at):
        def direct(d, n):
            return pltpu.make_async_remote_copy(
                source.at[at(0, n)], ref.at[me, at(0, n)], send.at[d, 0, n], recv.at[d, 0, n],
                device_id={"cols": ahead(d) * 2 + core}, device_id_type=MESH,
            )

        def relay(d, n):
            block = behind(d) * 2 + core
            return pltpu.make_async_remote_copy(
                source.at[at(0, n)] if d == 0 else ref.at[block, at(d, n)], ref.at[block, at(d, n)],
                send.at[d, 1, n], recv.at[d, 1, n],
                device_id={"cols": sibling}, device_id_type=MESH,
            )

        return direct, relay

    def group(d, n):
        return pl.ds(pl.multiple_of(behind(d + n) * (2 * width), 2 * width), 2 * width)

    direct, relay = copies(all_ref, own_ref, a_send, a_recv, lambda d, n: pl.ds(n * size, size))
    far_panel, near_panel = copies(gram_ref, gram_ref.at[me], d_send, d_recv, group)

    def multiply(block, ch):
        at = pl.ds(ch * size, size)
        to = pl.ds(pl.multiple_of(block * width, width), width)
        product = dot(all_ref[block, at, :], own_ref[at, :], 0, 0)
        if ch == 0:
            part[to, :] = product
        else:
            part[to, :] += product

    def rows_of(g, r):
        return pl.ds(pl.multiple_of(behind(g) * (2 * width) + r * piece, piece), piece)

    def scatter(g, k):
        return pltpu.make_async_remote_copy(
            part.at[rows_of(g, peer(k))], land.at[g, k - 1],
            b_send.at[g, k - 1], b_recv.at[g, k - 1],
            device_id={"rows": peer(k)}, device_id_type=MESH,
        )

    def spread(g, k):
        return pltpu.make_async_remote_copy(
            gram_ref.at[me, rows_of(g, row)], gram_ref.at[me, rows_of(g, row)],
            c_send.at[g, k - 1], c_recv.at[g, k - 1],
            device_id={"rows": peer(k)}, device_id_type=MESH,
        )

    def send_group(g):
        for k in range(1, nr):
            start(scatter(g, k))

    def sum_group(g):
        total = part[rows_of(g, row), :]
        for k in range(1, nr):
            scatter(g, k).wait_recv()
            total += land[g, k - 1]
        gram_ref[me, rows_of(g, row), :] = total
        for k in range(1, nr):
            start(spread(g, k))

    def share_group(g):
        for k in range(1, nr):
            spread(g, k).wait_recv()
        for d in far:
            start(far_panel(d, g))
        start(near_panel(0, g))

    for ch in range(chunks):
        for d in far:
            start(direct(d, ch))
    for ch in range(chunks):
        start(relay(0, ch))
    all_ref[me] = own_ref[...]
    for ch in range(chunks):
        multiply(me, ch)
    for ch in range(chunks):
        relay(0, ch).wait_recv()
        multiply(sibling, ch)
    send_group(0)
    for ch in range(chunks + 1):
        for d in far:
            if ch < chunks:
                direct(d, ch).wait_recv()
                start(relay(d, ch))
                multiply(behind(d) * 2 + core, ch)
            if ch > 0:
                relay(d, ch - 1).wait_recv()
                multiply(behind(d) * 2 + 1 - core, ch - 1)
        if ch == chunks - 2:
            sum_group(0)
    for g in far:
        send_group(g)
    share_group(0)
    for g in far:
        sum_group(g)
    for g in far:
        share_group(g)
    for g in range(chips):
        for d in far:
            far_panel(d, g).wait_recv()
            start(near_panel(d, g))
    for g in range(chips):
        for d in range(chips):
            near_panel(d, g).wait_recv()
    for copy in started:
        copy.wait_send()


def gather(nb, nr, snapshots):
    rows, width = snapshots.shape
    chips = nb // 2
    dma = pltpu.SemaphoreType.DMA
    return pl.pallas_call(
        functools.partial(gather_kernel, nb, nr),
        out_shape=(
            jax.ShapeDtypeStruct((nb, rows, width), jnp.float32),
            jax.ShapeDtypeStruct((nb, nb * width, width), jnp.float32),
        ),
        in_specs=[VMEM],
        out_specs=(VMEM, VMEM),
        scratch_shapes=[
            pltpu.VMEM((nb * width, width), jnp.float32),
            pltpu.VMEM((chips, nr - 1, 2 * width // nr, width), jnp.float32),
            dma((chips, 2, 4)), dma((chips, 2, 4)),
            dma((chips, nr - 1)), dma((chips, nr - 1)),
            dma((chips, nr - 1)), dma((chips, nr - 1)),
            dma((chips, 2, chips)), dma((chips, 2, chips)),
        ],
        compiler_params=pltpu.CompilerParams(
            collective_id=0, has_side_effects=True, vmem_limit_bytes=48 * 2**20
        ),
    )(snapshots)


def local(nb, nr, snapshots, plan):
    label = lax.axis_index("cols").astype(jnp.int32)
    blocks, gram = gather(nb, nr, snapshots)
    return rotate(nb, plan, label.reshape(1), gram, blocks)


def solution(mesh):
    return jax.shard_map(
        functools.partial(local, mesh.shape["cols"], mesh.shape["rows"]),
        mesh=mesh,
        in_specs=(P("rows", "cols"), P()),
        out_specs=P("rows", "cols"),
        check_vma=False,
    )
```

```python
import functools

import jax
import jax.numpy as jnp
from jax import lax
from jax.experimental import pallas as pl
from jax.experimental.pallas import tpu as pltpu
from jax.sharding import PartitionSpec as P

NSI = 5
EPS = 1e-6
VMEM = pl.BlockSpec(memory_space=pltpu.VMEM)
MESH = pl.DeviceIdType.MESH
SMEM = pl.BlockSpec(memory_space=pltpu.SMEM)


def split(x):
    high = x.astype(jnp.bfloat16)
    return high, (x - high.astype(jnp.float32)).astype(jnp.bfloat16)


def dots(a, b, ca=1, cb=0):
    def one(x, y):
        return lax.dot_general(
            x, y, (((ca,), (cb,)), ((), ())), preferred_element_type=jnp.float32
        )

    return one(a[0], b[0]) + (one(a[0], b[1]) + one(a[1], b[0]))


def dot(a, b, ca=1, cb=0):
    return dots(split(a), split(b), ca, cb)


def columns(gens):
    width = gens[0].shape[0]
    row = lax.broadcasted_iota(jnp.int32, (width, width), 0)
    col = lax.broadcasted_iota(jnp.int32, (width, width), 1)
    eye = jnp.where(row == col, 1.0, 0.0).astype(jnp.float32)
    parts = [split(g) for g in gens]
    zs = [0.5 * (eye + dots(p, p, 1, 1)) for p in parts]
    qs = None
    for index in range(NSI):
        ts = [1.5 * eye - 0.5 * z for z in zs]
        tsp = [split(t) for t in ts]
        if qs is None:
            qs = [t * (0.5**0.5) for t in ts]
        else:
            qs = [dots(split(q), t) for q, t in zip(qs, tsp)]
        if index < NSI - 1:
            squares = [dots(t, t) for t in tsp]
            zs = [dot(z, s) for z, s in zip(zs, squares)]
    return [(q, dots(p, split(q), 0, 0)) for q, p in zip(qs, parts)]


def generator(cross, own, other, sign):
    width = cross.shape[0]
    row = lax.broadcasted_iota(jnp.int32, (width, width), 0)
    col = lax.broadcasted_iota(jnp.int32, (width, width), 1)
    diag = row == col
    dc = jnp.sum(jnp.where(diag, own, 0.0), axis=1, keepdims=True)
    dp = jnp.sum(jnp.where(diag, other, 0.0), axis=0, keepdims=True)
    dc = jnp.maximum(dc, 0.0) + EPS
    dp = jnp.maximum(dp, 0.0) + EPS
    cross = cross * (lax.rsqrt(dc) * lax.rsqrt(dp))
    total = jnp.sum(jnp.sum(cross * cross, axis=1, keepdims=True), axis=0, keepdims=True)
    return cross * (sign * lax.rsqrt(1.0 + total))


def rotate(nb, plan_ref, label, gram_ref, all_ref, out_ref):
    width = out_ref.shape[1]
    masks = [plan_ref[s] for s in range(3)]
    labels = []
    for slot in range(8):
        block = label
        for bit in range(3):
            if slot >> bit & 1:
                block = jnp.bitwise_xor(block, masks[bit])
        labels.append(block)

    def sign(i, j):
        return jnp.where(labels[i] < labels[j], 1.0, -1.0).astype(jnp.float32)

    loaded = {}

    def gram(i, j):
        if (i, j) not in loaded:
            loaded[i, j] = gram_ref[labels[j], labels[i]]
        return loaded[i, j]

    def stack(parts, axis):
        return jnp.concatenate(parts, axis=axis)

    outs = (0, 2, 4, 6)
    gens = [generator(gram(i, i + 1), gram(i, i), gram(i + 1, i + 1), sign(i, i + 1)) for i in outs]
    first = columns(gens)
    col = {i: split(stack(c, 0)) for i, c in zip(outs, first)}
    after = {}
    for i in outs:
        for j in outs:
            if j < i:
                continue
            wide = stack(
                [stack([gram(i + p, j), gram(i + p, j + 1)], 1) for p in (0, 1)], 0
            )
            half = dots(split(wide), col[j])
            after[i, j] = dots(col[i], split(half), 0, 0)

    gens = [generator(after[i, i + 2], after[i, i], after[i + 2, i + 2], sign(i, i + 2)) for i in (0, 4)]
    second = columns(gens)
    c0, c4 = [split(stack(c, 0)) for c in second]

    def block(i, j):
        return stack(
            [
                stack([after[i, j], after[i, j + 2]], 1),
                stack([after[i + 2, j] if i + 2 <= j else after[j, i + 2].T, after[i + 2, j + 2]], 1),
            ],
            0,
        )

    def update(ci, mat, cj):
        return dots(ci, split(dots(split(mat), cj)), 0, 0)

    g00 = update(c0, block(0, 0), c0)
    g04 = update(c0, block(0, 4), c4)
    g44 = update(c4, block(4, 4), c4)
    gens = [generator(g04, g00, g44, sign(0, 4))]
    (a, b), = columns(gens)
    top = dots(c0, split(a))
    bottom = dots(c4, split(b))
    weight = {0: top[:width], 2: top[width:], 4: bottom[:width], 6: bottom[width:]}
    coef = {}
    for i in outs:
        both = dots(col[i], split(weight[i]))
        coef[i], coef[i + 1] = both[:width], both[width:]
    slots = range(8)
    if nb == 4:
        coef = {k: coef[k] + coef[7 - k] for k in range(4)}
        slots = range(4)
    coefs = [split(coef[k]) for k in slots]
    rows = out_ref.shape[0]
    tile = min(rows, 256)

    for at in range(0, rows, tile):
        total = jnp.zeros((tile, width), jnp.float32)
        for k in range(len(coefs)):
            total += dots(split(all_ref[labels[k], at : at + tile]), coefs[k])
        out_ref[at : at + tile, :] = total


def kernel(nb, nr, plan_ref, own_ref, out_ref, all_ref, gram_ref, part, land, *sems):
    a_send, a_recv, b_send, b_recv, c_send, c_recv, d_send, d_recv = sems
    me, row = lax.axis_index("cols"), lax.axis_index("rows")
    chips = nb // 2
    chip, core = me // 2, lax.rem(me, 2)
    sibling = chip * 2 + (1 - core)
    rows, width = own_ref.shape
    piece = 2 * width // nr
    far = range(1, chips)
    chunks = a_send.shape[2]
    size = rows // chunks

    def ahead(d):
        return lax.rem(chip + d, chips)

    def behind(d):
        return lax.rem(chip + 2 * chips - d, chips)

    def peer(k):
        return lax.rem(row + k, nr)

    barrier = pltpu.get_barrier_semaphore()
    targets = [{"cols": sibling}] + [{"cols": ahead(d) * 2 + core} for d in far]
    targets += [{"rows": peer(k)} for k in range(1, nr)]
    for target in targets:
        pl.semaphore_signal(barrier, inc=1, device_id=target, device_id_type=MESH)
    pl.semaphore_wait(barrier, len(targets))

    started = []

    def start(copy):
        copy.start()
        started.append(copy)

    def copies(ref, source, send, recv, at):
        def direct(d, n):
            return pltpu.make_async_remote_copy(
                source.at[at(0, n)], ref.at[me, at(0, n)], send.at[d, 0, n], recv.at[d, 0, n],
                device_id={"cols": ahead(d) * 2 + core}, device_id_type=MESH,
            )

        def relay(d, n):
            block = behind(d) * 2 + core
            return pltpu.make_async_remote_copy(
                source.at[at(0, n)] if d == 0 else ref.at[block, at(d, n)], ref.at[block, at(d, n)],
                send.at[d, 1, n], recv.at[d, 1, n],
                device_id={"cols": sibling}, device_id_type=MESH,
            )

        return direct, relay

    def group(d, n):
        return pl.ds(behind(d + n) * 2, 2)

    direct, relay = copies(all_ref, own_ref, a_send, a_recv, lambda d, n: pl.ds(n * size, size))
    far_panel, near_panel = copies(gram_ref, gram_ref.at[me], d_send, d_recv, group)

    def multiply(block, ch):
        at = pl.ds(ch * size, size)
        to = pl.ds(pl.multiple_of(block * width, width), width)
        product = dot(all_ref[block, at, :], own_ref[at, :], 0, 0)
        if ch == 0:
            part[to, :] = product
        else:
            part[to, :] += product

    def rows_of(g, r):
        return pl.ds(pl.multiple_of(behind(g) * (2 * width) + r * piece, piece), piece)

    def place(g):
        half = nr // 2
        at = pl.ds(pl.multiple_of(lax.rem(row, half) * piece, piece), piece)
        return gram_ref.at[me, behind(g) * 2 + row // half, at]

    def scatter(g, k):
        return pltpu.make_async_remote_copy(
            part.at[rows_of(g, peer(k))], land.at[g, k - 1],
            b_send.at[g, k - 1], b_recv.at[g, k - 1],
            device_id={"rows": peer(k)}, device_id_type=MESH,
        )

    def spread(g, k):
        return pltpu.make_async_remote_copy(
            place(g), place(g),
            c_send.at[g, k - 1], c_recv.at[g, k - 1],
            device_id={"rows": peer(k)}, device_id_type=MESH,
        )

    def send_group(g):
        for k in range(1, nr):
            start(scatter(g, k))

    def sum_group(g):
        total = part[rows_of(g, row), :]
        for k in range(1, nr):
            scatter(g, k).wait_recv()
            total += land[g, k - 1]
        place(g)[...] = total
        for k in range(1, nr):
            start(spread(g, k))

    def share_group(g):
        for k in range(1, nr):
            spread(g, k).wait_recv()
        for d in far:
            start(far_panel(d, g))
        start(near_panel(0, g))

    for ch in range(chunks):
        for d in far:
            start(direct(d, ch))
    for ch in range(chunks):
        start(relay(0, ch))
    all_ref[me] = own_ref[...]
    for ch in range(chunks):
        multiply(me, ch)
    for ch in range(chunks):
        relay(0, ch).wait_recv()
        multiply(sibling, ch)
    send_group(0)
    for ch in range(chunks + 1):
        for d in far:
            if ch < chunks:
                direct(d, ch).wait_recv()
                start(relay(d, ch))
                multiply(behind(d) * 2 + core, ch)
            if ch > 0:
                relay(d, ch - 1).wait_recv()
                multiply(behind(d) * 2 + 1 - core, ch - 1)
        if ch == chunks - 2:
            sum_group(0)
    for g in far:
        send_group(g)
    share_group(0)
    for g in far:
        sum_group(g)
    for g in far:
        share_group(g)
    for g in range(chips):
        for d in far:
            far_panel(d, g).wait_recv()
            start(near_panel(d, g))
    for g in range(chips):
        for d in range(chips):
            near_panel(d, g).wait_recv()
    rotate(nb, plan_ref, me, gram_ref, all_ref, out_ref)
    for copy in started:
        copy.wait_send()


def local(nb, nr, snapshots, plan):
    rows, width = snapshots.shape
    chips = nb // 2
    dma = pltpu.SemaphoreType.DMA
    return pl.pallas_call(
        functools.partial(kernel, nb, nr),
        out_shape=jax.ShapeDtypeStruct((rows, width), jnp.float32),
        in_specs=[SMEM, VMEM],
        out_specs=VMEM,
        scratch_shapes=[
            pltpu.VMEM((nb, rows, width), jnp.float32),
            pltpu.VMEM((nb, nb, width, width), jnp.float32),
            pltpu.VMEM((nb * width, width), jnp.float32),
            pltpu.VMEM((chips, nr - 1, 2 * width // nr, width), jnp.float32),
            dma((chips, 2, 4)), dma((chips, 2, 4)),
            dma((chips, nr - 1)), dma((chips, nr - 1)),
            dma((chips, nr - 1)), dma((chips, nr - 1)),
            dma((chips, 2, chips)), dma((chips, 2, chips)),
        ],
        compiler_params=pltpu.CompilerParams(
            collective_id=0, has_side_effects=True, vmem_limit_bytes=48 * 2**20
        ),
    )(plan, snapshots)


def solution(mesh):
    return jax.shard_map(
        functools.partial(local, mesh.shape["cols"], mesh.shape["rows"]),
        mesh=mesh,
        in_specs=(P("rows", "cols"), P()),
        out_specs=P("rows", "cols"),
        check_vma=False,
    )
```

```python
import functools

import jax
import jax.numpy as jnp
from jax import lax
from jax.experimental import pallas as pl
from jax.experimental.pallas import tpu as pltpu
from jax.sharding import PartitionSpec as P

NSI = 5
EPS = 1e-6
VMEM = pl.BlockSpec(memory_space=pltpu.VMEM)
MESH = pl.DeviceIdType.MESH
SMEM = pl.BlockSpec(memory_space=pltpu.SMEM)


def split(x):
    high = x.astype(jnp.bfloat16)
    return high, (x - high.astype(jnp.float32)).astype(jnp.bfloat16)


def dots(a, b, ca=1, cb=0):
    def one(x, y):
        return lax.dot_general(
            x, y, (((ca,), (cb,)), ((), ())), preferred_element_type=jnp.float32
        )

    return one(a[0], b[0]) + (one(a[0], b[1]) + one(a[1], b[0]))


def dot(a, b, ca=1, cb=0):
    return dots(split(a), split(b), ca, cb)


def columns(gens):
    width = gens[0].shape[0]
    row = lax.broadcasted_iota(jnp.int32, (width, width), 0)
    col = lax.broadcasted_iota(jnp.int32, (width, width), 1)
    eye = jnp.where(row == col, 1.0, 0.0).astype(jnp.float32)
    parts = [split(g) for g in gens]
    zs = [0.5 * (eye + dots(p, p, 1, 1)) for p in parts]
    qs = None
    for index in range(NSI):
        ts = [1.5 * eye - 0.5 * z for z in zs]
        tsp = [split(t) for t in ts]
        if qs is None:
            qs = [t * (0.5**0.5) for t in ts]
        else:
            qs = [dots(split(q), t) for q, t in zip(qs, tsp)]
        if index < NSI - 1:
            squares = [dots(t, t) for t in tsp]
            zs = [dot(z, s) for z, s in zip(zs, squares)]
    return [(q, dots(p, split(q), 0, 0)) for q, p in zip(qs, parts)]


def generator(cross, own, other, sign):
    width = cross.shape[0]
    row = lax.broadcasted_iota(jnp.int32, (width, width), 0)
    col = lax.broadcasted_iota(jnp.int32, (width, width), 1)
    diag = row == col
    dc = jnp.sum(jnp.where(diag, own, 0.0), axis=1, keepdims=True)
    dp = jnp.sum(jnp.where(diag, other, 0.0), axis=0, keepdims=True)
    dc = jnp.maximum(dc, 0.0) + EPS
    dp = jnp.maximum(dp, 0.0) + EPS
    cross = cross * (lax.rsqrt(dc) * lax.rsqrt(dp))
    total = jnp.sum(jnp.sum(cross * cross, axis=1, keepdims=True), axis=0, keepdims=True)
    return cross * (sign * lax.rsqrt(1.0 + total))


def rotate(nb, plan_ref, label, gram_ref, all_ref, out_ref):
    width = out_ref.shape[1]
    masks = [plan_ref[s] for s in range(3)]
    labels = []
    for slot in range(8):
        block = label
        for bit in range(3):
            if slot >> bit & 1:
                block = jnp.bitwise_xor(block, masks[bit])
        labels.append(block)

    def sign(i, j):
        return jnp.where(labels[i] < labels[j], 1.0, -1.0).astype(jnp.float32)

    loaded = {}

    def gram(i, j):
        if (i, j) not in loaded:
            loaded[i, j] = gram_ref[labels[j], labels[i]]
        return loaded[i, j]

    def stack(parts, axis):
        return jnp.concatenate(parts, axis=axis)

    outs = (0, 2, 4, 6)
    gens = [generator(gram(i, i + 1), gram(i, i), gram(i + 1, i + 1), sign(i, i + 1)) for i in outs]
    first = columns(gens)
    col = {i: split(stack(c, 0)) for i, c in zip(outs, first)}
    after = {}
    for i in outs:
        for j in outs:
            if j < i:
                continue
            wide = stack(
                [stack([gram(i + p, j), gram(i + p, j + 1)], 1) for p in (0, 1)], 0
            )
            half = dots(split(wide), col[j])
            after[i, j] = dots(col[i], split(half), 0, 0)

    gens = [generator(after[i, i + 2], after[i, i], after[i + 2, i + 2], sign(i, i + 2)) for i in (0, 4)]
    second = columns(gens)
    c0, c4 = [split(stack(c, 0)) for c in second]

    def block(i, j):
        return stack(
            [
                stack([after[i, j], after[i, j + 2]], 1),
                stack([after[i + 2, j] if i + 2 <= j else after[j, i + 2].T, after[i + 2, j + 2]], 1),
            ],
            0,
        )

    def update(ci, mat, cj):
        return dots(ci, split(dots(split(mat), cj)), 0, 0)

    g00 = update(c0, block(0, 0), c0)
    g04 = update(c0, block(0, 4), c4)
    g44 = update(c4, block(4, 4), c4)
    gens = [generator(g04, g00, g44, sign(0, 4))]
    (a, b), = columns(gens)
    top = dots(c0, split(a))
    bottom = dots(c4, split(b))
    weight = {0: top[:width], 2: top[width:], 4: bottom[:width], 6: bottom[width:]}
    coef = {}
    for i in outs:
        both = dots(col[i], split(weight[i]))
        coef[i], coef[i + 1] = both[:width], both[width:]
    slots = range(8)
    if nb == 4:
        coef = {k: coef[k] + coef[7 - k] for k in range(4)}
        slots = range(4)
    coefs = [split(coef[k]) for k in slots]
    rows = out_ref.shape[0]
    tile = min(rows, 256)

    for at in range(0, rows, tile):
        total = jnp.zeros((tile, width), jnp.float32)
        for k in range(len(coefs)):
            total += dots(split(all_ref[labels[k], at : at + tile]), coefs[k])
        out_ref[at : at + tile, :] = total


def kernel(nb, nr, plan_ref, own_ref, out_ref, all_ref, gram_ref, part, land, own_sem, *sems):
    a_send, a_recv, b_send, b_recv, c_send, c_recv, d_send, d_recv = sems
    me, row = lax.axis_index("cols"), lax.axis_index("rows")
    chips = nb // 2
    chip, core = me // 2, lax.rem(me, 2)
    sibling = chip * 2 + (1 - core)
    rows, width = own_ref.shape
    piece = 2 * width // nr
    far = range(1, chips)
    chunks = a_send.shape[2]
    size = rows // chunks

    def ahead(d):
        return lax.rem(chip + d, chips)

    def behind(d):
        return lax.rem(chip + 2 * chips - d, chips)

    def peer(k):
        return lax.rem(row + k, nr)

    fetch = pltpu.make_async_copy(own_ref, all_ref.at[me], own_sem)
    fetch.start()
    barrier = pltpu.get_barrier_semaphore()
    targets = [{"cols": sibling}] + [{"cols": ahead(d) * 2 + core} for d in far]
    targets += [{"rows": peer(k)} for k in range(1, nr)]
    for target in targets:
        pl.semaphore_signal(barrier, inc=1, device_id=target, device_id_type=MESH)
    pl.semaphore_wait(barrier, len(targets))

    started = []

    def start(copy):
        copy.start()
        started.append(copy)

    def copies(ref, source, send, recv, at):
        def direct(d, n):
            return pltpu.make_async_remote_copy(
                source.at[at(0, n)], ref.at[me, at(0, n)], send.at[d, 0, n], recv.at[d, 0, n],
                device_id={"cols": ahead(d) * 2 + core}, device_id_type=MESH,
            )

        def relay(d, n):
            block = behind(d) * 2 + core
            return pltpu.make_async_remote_copy(
                source.at[at(0, n)] if d == 0 else ref.at[block, at(d, n)], ref.at[block, at(d, n)],
                send.at[d, 1, n], recv.at[d, 1, n],
                device_id={"cols": sibling}, device_id_type=MESH,
            )

        return direct, relay

    def group(d, n):
        return pl.ds(behind(d + n) * 2, 2)

    direct, relay = copies(all_ref, own_ref, a_send, a_recv, lambda d, n: pl.ds(n * size, size))
    far_panel, near_panel = copies(gram_ref, gram_ref.at[me], d_send, d_recv, group)

    def multiply(block, ch):
        at = pl.ds(ch * size, size)
        to = pl.ds(pl.multiple_of(block * width, width), width)
        product = dot(all_ref[block, at, :], all_ref[me, at, :], 0, 0)
        if ch == 0:
            part[to, :] = product
        else:
            part[to, :] += product

    def rows_of(g, r):
        return pl.ds(pl.multiple_of(behind(g) * (2 * width) + r * piece, piece), piece)

    def place(g):
        half = nr // 2
        at = pl.ds(pl.multiple_of(lax.rem(row, half) * piece, piece), piece)
        return gram_ref.at[me, behind(g) * 2 + row // half, at]

    def scatter(g, k):
        return pltpu.make_async_remote_copy(
            part.at[rows_of(g, peer(k))], land.at[g, k - 1],
            b_send.at[g, k - 1], b_recv.at[g, k - 1],
            device_id={"rows": peer(k)}, device_id_type=MESH,
        )

    def spread(g, k):
        return pltpu.make_async_remote_copy(
            place(g), place(g),
            c_send.at[g, k - 1], c_recv.at[g, k - 1],
            device_id={"rows": peer(k)}, device_id_type=MESH,
        )

    def send_group(g):
        for k in range(1, nr):
            start(scatter(g, k))

    def sum_group(g):
        total = part[rows_of(g, row), :]
        for k in range(1, nr):
            scatter(g, k).wait_recv()
            total += land[g, k - 1]
        place(g)[...] = total
        for k in range(1, nr):
            start(spread(g, k))

    def share_group(g):
        for k in range(1, nr):
            spread(g, k).wait_recv()
        for d in far:
            start(far_panel(d, g))
        start(near_panel(0, g))

    for ch in range(chunks):
        for d in far:
            start(direct(d, ch))
    for ch in range(chunks):
        start(relay(0, ch))
    fetch.wait()
    for ch in range(chunks):
        multiply(me, ch)
    for ch in range(chunks):
        relay(0, ch).wait_recv()
        multiply(sibling, ch)
    send_group(0)
    for ch in range(chunks + 1):
        for d in far:
            if ch < chunks:
                direct(d, ch).wait_recv()
                start(relay(d, ch))
                multiply(behind(d) * 2 + core, ch)
            if ch > 0:
                relay(d, ch - 1).wait_recv()
                multiply(behind(d) * 2 + 1 - core, ch - 1)
        if ch == chunks - 2:
            sum_group(0)
    for g in far:
        send_group(g)
    share_group(0)
    for g in far:
        sum_group(g)
    for g in far:
        share_group(g)
    for g in range(chips):
        for d in far:
            far_panel(d, g).wait_recv()
            start(near_panel(d, g))
    for g in range(chips):
        for d in range(chips):
            near_panel(d, g).wait_recv()
    rotate(nb, plan_ref, me, gram_ref, all_ref, out_ref)
    for copy in started:
        copy.wait_send()


def local(nb, nr, snapshots, plan):
    rows, width = snapshots.shape
    chips = nb // 2
    dma = pltpu.SemaphoreType.DMA
    return pl.pallas_call(
        functools.partial(kernel, nb, nr),
        out_shape=jax.ShapeDtypeStruct((rows, width), jnp.float32),
        in_specs=[SMEM, pl.BlockSpec(memory_space=pl.ANY)],
        out_specs=VMEM,
        scratch_shapes=[
            pltpu.VMEM((nb, rows, width), jnp.float32),
            pltpu.VMEM((nb, nb, width, width), jnp.float32),
            pltpu.VMEM((nb * width, width), jnp.float32),
            pltpu.VMEM((chips, nr - 1, 2 * width // nr, width), jnp.float32),
            dma,
            dma((chips, 2, 4)), dma((chips, 2, 4)),
            dma((chips, nr - 1)), dma((chips, nr - 1)),
            dma((chips, nr - 1)), dma((chips, nr - 1)),
            dma((chips, 2, chips)), dma((chips, 2, chips)),
        ],
        compiler_params=pltpu.CompilerParams(
            collective_id=0, has_side_effects=True, vmem_limit_bytes=48 * 2**20
        ),
    )(plan, snapshots)


def solution(mesh):
    return jax.shard_map(
        functools.partial(local, mesh.shape["cols"], mesh.shape["rows"]),
        mesh=mesh,
        in_specs=(P("rows", "cols"), P()),
        out_specs=P("rows", "cols"),
        check_vma=False,
    )
```
